768 devices in a mesh: stn: 32 (over z_lo, x, core), tm: 24 (over z_hi, y).
Axes of the slice: x: 4, y: 8, z: 12 (z_hi: 3, z_lo: 4; z = z_hi * 4 + z_lo), core: 2. Of those that a mesh axis runs over, the one named last changes fastest.
Arguments:
- samples: bfloat16 [2, 64, 96, 4096], P(None, 'stn', 'tm'), may hold values from -6 to 6
- valid_spectra: int32 [24], P('tm'), may hold values from 1 to 4, as said below
- root_blocks: int32 [4], replicated, may hold values from 0 to 31, as said below
Outputs:
- visibilities: float32 [24, 2, 4, 64, 2, 4096], P('tm', None, None, 'stn')
The draws below stay inside these ranges and needn't reach their ends.
Inputs may be any that keep to these rules, and one draw needn't show every extreme that they name: `valid_spectra`: every value from 1 to 4; some time block has exactly 4, some exactly 1. `root_blocks`: 4 different station blocks, in an order drawn from the seed; block 0 and block 32 - 1 are always among them.
All inputs are finite; a program needn't handle non-finite values.
Results may differ from the reference program's by a relative error of at most 0.004.
Values may be sent and summed in bfloat16 or wider, within the bound.
No kernel may reach another device: no remote copies, remote signals or barrier semaphores. Data moves between devices by JAX's collectives and lax.ppermute only.
A program may use at most 32 MiB of HBM per device.

```python
import math
import jax
import jax.numpy as jnp
from jax import lax

F = 4096
TAPS = 4
STEPS = 4
P_SIZE = 2
M = 4
INPUTS = 64
FRAMES = 96
N_STN = 32
N_TM = 24


def draw_valid_spectra(key, part):
    values = jax.random.randint(jax.random.fold_in(key, 1), (N_TM,), M // 4, M + 1)
    order = jax.random.permutation(jax.random.fold_in(key, 2), N_TM)
    values = values.at[order[0]].set(M)
    values = values.at[order[1]].set(M // 4)
    return values.astype(jnp.int32)


def draw_root_blocks(key, part):
    middle = jax.random.permutation(jax.random.fold_in(key, 3), N_STN - 2)[:STEPS - 2] + 1
    chosen = jnp.concatenate([jnp.array([0, N_STN - 1], jnp.int32), middle.astype(jnp.int32)])
    return jax.random.permutation(jax.random.fold_in(key, 4), chosen).astype(jnp.int32)


def level_of(key, dims, pieces, low, top_value):
    def one(position, shards_of):
        heights = jax.random.uniform(jax.random.fold_in(jax.random.fold_in(key, 6), position), (shards_of,), jnp.float32, low / len(pieces), top_value / len(pieces))
        return jnp.repeat(jnp.exp(heights), dims[position] // shards_of).reshape((-1,) + (1,) * (len(dims) - position - 1))

    gain = one(*pieces[0])
    for cut in pieces[1:]:
        gain = gain * one(*cut)
    return gain


def normal_values(own_key, dims, spread, most, shards=(), held_as=jnp.bfloat16):
    values = jax.random.normal(own_key, dims, jnp.float32) * spread
    if len(shards) > 0:
        values = level_of(own_key, dims, shards, -0.22, 0.18) * values
    return jnp.clip(values, min=-most, max=most).astype(held_as)


def setup_inputs(seed: int = 0) -> dict:
    keys = jax.random.split(jax.random.key(seed), 4)
    return {
        "samples": normal_values(keys[0], (2, INPUTS, FRAMES, F), 1.0, 6.0, ((1, 32), (2, 24))),
        "valid_spectra": draw_valid_spectra(jax.random.fold_in(keys[3], 71), 0),
        "root_blocks": draw_root_blocks(jax.random.fold_in(keys[3], 71), 0),
    }


def prototype(channels, taps):
    positions = jnp.arange(taps * channels, dtype=jnp.float32)
    middle = (positions - 0.5 * taps * channels + 0.5) / channels
    window = 0.5 - 0.5 * jnp.cos(2.0 * math.pi * (positions + 0.5) / (taps * channels))
    return (jnp.sinc(middle) * window).reshape(taps, channels)

def filtered(extended, taps_table, frames):
    running = jnp.zeros(extended.shape[:2] + (frames, extended.shape[3]), jnp.float32)
    for tap_index in range(taps_table.shape[0]):
        running = running + taps_table[tap_index] * extended[:, :, tap_index:tap_index + frames].astype(jnp.float32)
    return running

def reference(samples, valid_spectra, root_blocks):
    taps_table = prototype(F, TAPS)
    blocks = samples.reshape(2, INPUTS, N_TM, M, F)
    norm_scale = 1.0 / math.sqrt(F)

    def one_block(block_index):
        own = lax.dynamic_index_in_dim(blocks, block_index, 2, keepdims=False)
        previous = lax.dynamic_index_in_dim(blocks, jnp.maximum(block_index - 1, 0), 2, keepdims=False)
        history = previous[:, :, M - (TAPS - 1):] * (block_index > 0).astype(samples.dtype)
        extended = jnp.concatenate([history, own], axis=2)
        filt = filtered(extended, taps_table, M)
        spectrum = jnp.fft.fft(filt[0] + 1j * filt[1], axis=-1) * norm_scale
        spec_real = spectrum.real.astype(jnp.bfloat16).astype(jnp.float32)
        spec_imag = spectrum.imag.astype(jnp.bfloat16).astype(jnp.float32)
        valid_count = valid_spectra[block_index]
        usable = (jnp.arange(M) < valid_count).astype(jnp.float32)
        own_real = spec_real * usable[None, :, None]
        own_imag = spec_imag * usable[None, :, None]
        outputs = []
        for step_index in range(STEPS):
            start = (root_blocks[step_index] * P_SIZE).astype(jnp.int32)
            far_real = lax.dynamic_slice_in_dim(spec_real, start, P_SIZE, 0)
            far_imag = lax.dynamic_slice_in_dim(spec_imag, start, P_SIZE, 0)
            vis_real = jnp.einsum('ijc,qjc->iqc', own_real, far_real) + jnp.einsum('ijc,qjc->iqc', own_imag, far_imag)
            vis_imag = jnp.einsum('ijc,qjc->iqc', own_imag, far_real) - jnp.einsum('ijc,qjc->iqc', own_real, far_imag)
            outputs.append(jnp.stack([vis_real, vis_imag]) / valid_count.astype(jnp.float32))
        return jnp.stack(outputs, axis=1)
    return lax.map(one_block, jnp.arange(N_TM, dtype=jnp.int32))
```

```python
import math

import jax
import jax.numpy as jnp
import ml_dtypes
import numpy as np
from jax import lax
from jax.experimental import pallas as pl
from jax.experimental.pallas import tpu as pltpu
from jax.sharding import PartitionSpec as P

TAPS = 4
STEPS = 4
ROWS = 32
COLS = 128
F32, BF16 = jnp.float32, jnp.bfloat16
VMEM = pl.BlockSpec(memory_space=pltpu.VMEM)
SMEM = pl.BlockSpec(memory_space=pltpu.SMEM)


def split(table):
    high = table.astype(ml_dtypes.bfloat16)
    low = (table - high.astype(np.float64)).astype(ml_dtypes.bfloat16)
    return high, low


def tables(channels):
    position = np.arange(TAPS * channels, dtype=np.float64)
    middle = (position - 0.5 * TAPS * channels + 0.5) / channels
    window = 0.5 - 0.5 * np.cos(2.0 * np.pi * (position + 0.5) / (TAPS * channels))
    taps = (np.sinc(middle) * window).astype(np.float32).reshape(TAPS * ROWS, COLS)
    row, col = np.arange(ROWS), np.arange(COLS)
    angle = 2.0 * np.pi * (row[:, None] * row[None, :] % ROWS) / ROWS
    cos, sin = np.cos(angle), np.sin(angle)
    high, low = split(np.block([[cos, sin], [-sin, cos]]))
    first = np.concatenate([high, high, low], axis=1)
    angle = 2.0 * np.pi * (row[:, None] * col[None, :]) / channels
    twist = np.concatenate([np.cos(angle), np.sin(angle)]).astype(np.float32)
    out_col = (4 * np.arange(32)[None, :] + np.arange(4)[:, None]).reshape(-1)
    angle = 2.0 * np.pi * (out_col[:, None] * col[None, :] % COLS) / COLS
    scale = 1.0 / math.sqrt(channels)
    cos, sin = np.cos(angle) * scale, np.sin(angle) * scale
    high, low = split(np.block([[cos, sin], [-sin, cos]]))
    second = np.concatenate([high, high, low], axis=1)
    return taps, first, twist, second


def spectra_kernel(own, past, taps, first, twist, second, by_tile, by_row, ext, mixed):
    for part in range(2):
        for sig in range(2):
            base = (part * 2 + sig) * ROWS * 8
            before = past[part, sig].astype(F32)
            now = own[part, sig].astype(F32)
            for tile in range(ROWS):
                lanes = slice(tile * COLS, (tile + 1) * COLS)
                ext[base + tile * 8 : base + tile * 8 + 4, :] = before[:, lanes]
                ext[base + tile * 8 + 4 : base + tile * 8 + 8, :] = now[:, lanes]
    weights = [taps[k * ROWS : (k + 1) * ROWS, :] for k in range(TAPS)]
    columns = []
    for sig in range(2):
        both = []
        for part in range(2):
            base = (part * 2 + sig) * ROWS * 8
            frame = [None] + [ext[pl.ds(base + r, ROWS, stride=8), :] for r in range(1, 8)]
            both.append(
                [
                    weights[0] * frame[j + 1]
                    + weights[1] * frame[j + 2]
                    + weights[2] * frame[j + 3]
                    + weights[3] * frame[j + 4]
                    for j in range(4)
                ]
            )
        for j in range(4):
            columns.append(jnp.concatenate([both[0][j], both[1][j]], axis=0))
    filt = jnp.concatenate(columns, axis=1)
    high = filt.astype(BF16)
    low = (filt - high.astype(F32)).astype(BF16)
    mid = jnp.dot(
        first[...], jnp.concatenate([high, low, high], axis=0), preferred_element_type=F32
    )
    cos, sin = twist[:ROWS, :], twist[ROWS:, :]
    turned = []
    for sj in range(8):
        real = mid[:ROWS, sj * COLS : (sj + 1) * COLS]
        imag = mid[ROWS:, sj * COLS : (sj + 1) * COLS]
        turned.append(jnp.concatenate([real * cos + imag * sin, imag * cos - real * sin], axis=1))
    turned = jnp.concatenate(turned, axis=0)
    high = turned.astype(BF16)
    low = (turned - high.astype(F32)).astype(BF16)
    out = lax.dot_general(
        second[...],
        jnp.concatenate([high, low, high], axis=1),
        (((1,), (1,)), ((), ())),
        preferred_element_type=F32,
    )
    quarter = lax.broadcasted_iota(jnp.int32, (ROWS, COLS), 1) // ROWS
    for part in range(2):
        for half in range(2):
            block = [
                out[(part * 4 + r) * 32 : (part * 4 + r + 1) * 32, half * 128 : (half + 1) * 128]
                for r in range(4)
            ]
            for b in range(4):
                moved = [
                    block[r] if r == b else pltpu.roll(block[r], 32 * ((r - b) % 4), 1)
                    for r in range(4)
                ]
                spec = jnp.where(
                    quarter < 2,
                    jnp.where(quarter == 0, moved[0], moved[1]),
                    jnp.where(quarter == 2, moved[2], moved[3]),
                )
                index = part * 8 + half * 4 + b
                by_row[index * 32 : (index + 1) * 32, :] = spec.astype(BF16)
                mixed[pl.ds(index, 32, stride=16), :] = spec
    by_tile[...] = mixed[...].astype(BF16)


def spectra(own, past):
    channels = own.shape[3]
    consts = [jnp.asarray(t) for t in tables(channels)]
    return pl.pallas_call(
        spectra_kernel,
        out_shape=[jax.ShapeDtypeStruct((512, COLS), BF16)] * 2,
        in_specs=[VMEM] * 6,
        out_specs=[VMEM] * 2,
        scratch_shapes=[pltpu.VMEM((4 * ROWS * 8, COLS), F32), pltpu.VMEM((512, COLS), F32)],
        compiler_params=pltpu.CompilerParams(vmem_limit_bytes=32 << 20),
        cost_estimate=pl.CostEstimate(flops=120_000_000, bytes_accessed=900_000, transcendentals=0),
    )(own, past, *consts)


def pick_kernel(peers, roots, pieces, out):
    for k in range(STEPS):
        piece = pieces[pl.ds(pl.multiple_of(roots[k] * 16, 16), 16), :]
        for peer in range(peers):
            out[peer * 64 + k * 16 : peer * 64 + (k + 1) * 16, :] = piece


def pick(roots, pieces, peers):
    return pl.pallas_call(
        lambda *refs: pick_kernel(peers, *refs),
        out_shape=jax.ShapeDtypeStruct((peers * 64, COLS), BF16),
        in_specs=[SMEM, VMEM],
        out_specs=VMEM,
        compiler_params=pltpu.CompilerParams(vmem_limit_bytes=32 << 20),
        cost_estimate=pl.CostEstimate(flops=0, bytes_accessed=400_000, transcendentals=0),
    )(roots, pieces)


def correlate_kernel(valid, core, own, near, far, out, mine, theirs):
    for place, block in ((core[0], near), (1 - core[0], far)):
        for peer in range(16):
            start = pl.multiple_of((2 * peer + place) * 64, 64)
            theirs[pl.ds(start, 64), :] = block[peer * 64 : (peer + 1) * 64, :].astype(F32)
    count = valid[0]
    weight = 1.0 / jnp.full((8, COLS), count, jnp.int32).astype(F32)
    nothing = jnp.zeros((8, COLS), F32)
    for j in range(4):
        scale = jnp.concatenate([jnp.where(j < count, weight, nothing)] * 4, axis=0)
        for ps in range(4):
            rows = slice((ps * 4 + j) * 32, (ps * 4 + j + 1) * 32)
            mine[rows, :] = own[rows, :].astype(F32) * scale
    for block in range(4):
        left = [
            mine[i * 32 + block * 8 : i * 32 + block * 8 + 8, :] for i in range(16)
        ]
        for k in range(STEPS):
            for q in range(2):
                start = block * 8 * 64 + k * 16 + q * 4
                real = [theirs[pl.ds(start + j, 8, stride=64), :] for j in range(4)]
                imag = [theirs[pl.ds(start + 8 + j, 8, stride=64), :] for j in range(4)]
                for s in range(2):
                    vis_real, vis_imag = nothing, nothing
                    for j in range(4):
                        a, b = left[s * 4 + j], left[8 + s * 4 + j]
                        vis_real = vis_real + (a * real[j] + b * imag[j])
                        vis_imag = vis_imag + (b * real[j] - a * imag[j])
                    at = (k * 2 + s) * 64 + block * 16 + q
                    out[pl.ds(at, 8, stride=2), :] = vis_real
                    out[pl.ds(512 + at, 8, stride=2), :] = vis_imag


def correlate(valid, core, own, near, far):
    return pl.pallas_call(
        correlate_kernel,
        out_shape=jax.ShapeDtypeStruct((1024, COLS), F32),
        in_specs=[SMEM, SMEM, VMEM, VMEM, VMEM],
        out_specs=VMEM,
        scratch_shapes=[pltpu.VMEM((512, COLS), F32), pltpu.VMEM((2048, COLS), F32)],
        compiler_params=pltpu.CompilerParams(vmem_limit_bytes=32 << 20),
        cost_estimate=pl.CostEstimate(flops=4_000_000, bytes_accessed=1_200_000, transcendentals=0),
    )(valid, core, own, near, far)


def local(samples, valid_spectra, root_blocks):
    blocks, places = lax.axis_size("tm"), lax.axis_size("stn")
    past = lax.ppermute(samples, "tm", [(b, b + 1) for b in range(blocks - 1)])
    by_tile, by_row = spectra(samples, past)
    pieces = lax.all_to_all(by_tile, "stn", 0, 0, tiled=True)
    picked = pick(root_blocks, pieces, places // 2)
    same_core = [[2 * p + c for p in range(places // 2)] for c in range(2)]
    near = lax.all_to_all(picked, "stn", 0, 0, axis_index_groups=same_core, tiled=True)
    far = lax.ppermute(near, "stn", [(d, d ^ 1) for d in range(places)])
    core = (lax.axis_index("stn") % 2).astype(jnp.int32).reshape(1)
    vis = correlate(valid_spectra, core, by_row, near, far)
    vis = vis.reshape(2, STEPS, 2, 32, 2, COLS).transpose(0, 1, 2, 4, 3, 5)
    return vis.reshape(1, 2, STEPS, 2, 2, 32 * COLS)


def solution(mesh):
    return jax.shard_map(
        local,
        mesh=mesh,
        in_specs=(P(None, "stn", "tm", None), P("tm"), P()),
        out_specs=P("tm", None, None, "stn", None, None),
        check_vma=False,
    )
```

```python
import math

import jax
import jax.numpy as jnp
import ml_dtypes
import numpy as np
from jax import lax
from jax.experimental import pallas as pl
from jax.experimental.pallas import tpu as pltpu
from jax.sharding import PartitionSpec as P

TAPS = 4
STEPS = 4
ROWS = 32
COLS = 128
F32, BF16 = jnp.float32, jnp.bfloat16
VMEM = pl.BlockSpec(memory_space=pltpu.VMEM)
SMEM = pl.BlockSpec(memory_space=pltpu.SMEM)
HBM = pl.BlockSpec(memory_space=pltpu.HBM)


def split(table):
    high = table.astype(ml_dtypes.bfloat16)
    low = (table - high.astype(np.float64)).astype(ml_dtypes.bfloat16)
    return high, low


def tables(channels):
    position = np.arange(TAPS * channels, dtype=np.float64)
    middle = (position - 0.5 * TAPS * channels + 0.5) / channels
    window = 0.5 - 0.5 * np.cos(2.0 * np.pi * (position + 0.5) / (TAPS * channels))
    taps = (np.sinc(middle) * window).astype(np.float32).reshape(TAPS * ROWS, COLS)
    row, col = np.arange(ROWS), np.arange(COLS)
    angle = 2.0 * np.pi * (row[:, None] * row[None, :] % ROWS) / ROWS
    cos, sin = np.cos(angle), np.sin(angle)
    high, low = split(np.block([[cos, sin], [-sin, cos]]))
    first = np.concatenate([high, high, low], axis=1)
    angle = 2.0 * np.pi * (row[:, None] * col[None, :]) / channels
    twist = np.concatenate([np.cos(angle), np.sin(angle)]).astype(np.float32)
    out_col = (4 * np.arange(32)[None, :] + np.arange(4)[:, None]).reshape(-1)
    angle = 2.0 * np.pi * (out_col[:, None] * col[None, :] % COLS) / COLS
    scale = 1.0 / math.sqrt(channels)
    cos, sin = np.cos(angle) * scale, np.sin(angle) * scale
    high, low = split(np.block([[cos, sin], [-sin, cos]]))
    second = np.concatenate([high, high, low], axis=1)
    return taps, first, twist, second


def tails_kernel(samples, tails, rows, held, mixed, sems):
    copies = [
        pltpu.make_async_copy(samples.at[part, sig], held.at[part, sig], sems.at[part * 2 + sig])
        for part in range(2)
        for sig in range(2)
    ]
    for copy in copies:
        copy.start()
    for part in range(2):
        copies[part * 2].wait()
        copies[part * 2 + 1].wait()
        both = jnp.concatenate(
            [held[part, 0].astype(F32), held[part, 1].astype(F32)], axis=0
        )
        for tile in range(ROWS):
            start = (part * ROWS + tile) * 8
            mixed[start : start + 8, :] = both[:, tile * COLS : (tile + 1) * COLS]
        for sig in range(2):
            for frame in range(4):
                row = mixed[pl.ds(part * ROWS * 8 + sig * 4 + frame, ROWS, stride=8), :]
                index = part * 2 + sig
                rows[(index * 4 + frame) * 32 : (index * 4 + frame + 1) * 32, :] = row
                if frame > 0:
                    start = (index * 3 + frame - 1) * 32
                    tails[start : start + 32, :] = row.astype(BF16)


def tails_of(samples):
    return pl.pallas_call(
        tails_kernel,
        out_shape=[
            jax.ShapeDtypeStruct((384, COLS), BF16),
            jax.ShapeDtypeStruct((512, COLS), F32),
        ],
        in_specs=[HBM],
        out_specs=[VMEM] * 2,
        scratch_shapes=[
            pltpu.VMEM(samples.shape, BF16),
            pltpu.VMEM((512, COLS), F32),
            pltpu.SemaphoreType.DMA((4,)),
        ],
        compiler_params=pltpu.CompilerParams(vmem_limit_bytes=32 << 20),
        cost_estimate=pl.CostEstimate(flops=0, bytes_accessed=600_000, transcendentals=0),
    )(samples)


def ready_kernel(rows, valid, roots, taps, first, twist, second, part_sums, *rest):
    near, numbers, sems = rest[:4], rest[4], rest[5]
    copies = [
        pltpu.make_async_copy(table, place, sems.at[i])
        for i, (table, place) in enumerate(zip((taps, first, twist, second), near))
    ]
    for copy in copies:
        copy.start()
    for k in range(STEPS):
        numbers[k] = roots[k]
    numbers[STEPS] = valid[0]
    numbers[STEPS + 1] = lax.rem(lax.axis_index("stn"), 2)
    copies[0].wait()
    weights = [near[0][k * ROWS : (k + 1) * ROWS, :] for k in range(TAPS)]
    for index in range(4):
        frame = [rows[(index * 4 + f) * 32 : (index * 4 + f + 1) * 32, :] for f in range(4)]
        for j in range(4):
            total = weights[3 - j] * frame[0]
            for f in range(1, j + 1):
                total = total + weights[3 - j + f] * frame[f]
            part_sums[(index * 4 + j) * 32 : (index * 4 + j + 1) * 32, :] = total
    for copy in copies[1:]:
        copy.wait()


def ready(rows, valid, roots, channels):
    consts = [jnp.asarray(t) for t in tables(channels)]
    return pl.pallas_call(
        ready_kernel,
        out_shape=[jax.ShapeDtypeStruct((512, COLS), F32)]
        + [jax.ShapeDtypeStruct(c.shape, c.dtype) for c in consts]
        + [jax.ShapeDtypeStruct((STEPS + 2,), jnp.int32)],
        in_specs=[VMEM, SMEM, SMEM] + [HBM] * 4,
        out_specs=[VMEM] * 5 + [SMEM],
        scratch_shapes=[pltpu.SemaphoreType.DMA((4,))],
        compiler_params=pltpu.CompilerParams(vmem_limit_bytes=32 << 20),
        cost_estimate=pl.CostEstimate(flops=700_000, bytes_accessed=900_000, transcendentals=0),
    )(rows, valid, roots, *consts)


def spectra_kernel(past, part_sums, taps, first, twist, second, by_tile, by_row, mixed):
    weights = [taps[k * ROWS : (k + 1) * ROWS, :] for k in range(TAPS)]
    columns = []
    for sig in range(2):
        both = []
        for part in range(2):
            index = part * 2 + sig
            frame = [
                past[(index * 3 + f) * 32 : (index * 3 + f + 1) * 32, :].astype(F32)
                for f in range(3)
            ]
            sums = [
                part_sums[(index * 4 + j) * 32 : (index * 4 + j + 1) * 32, :] for j in range(4)
            ]
            for j in range(3):
                for k in range(3 - j):
                    sums[j] = sums[j] + weights[k] * frame[j + k]
            both.append(sums)
        for j in range(4):
            columns.append(jnp.concatenate([both[0][j], both[1][j]], axis=0))
    filt = jnp.concatenate(columns, axis=1)
    high = filt.astype(BF16)
    low = (filt - high.astype(F32)).astype(BF16)
    mid = jnp.dot(
        first[...], jnp.concatenate([high, low, high], axis=0), preferred_element_type=F32
    )
    cos, sin = twist[:ROWS, :], twist[ROWS:, :]
    turned = []
    for sj in range(8):
        real = mid[:ROWS, sj * COLS : (sj + 1) * COLS]
        imag = mid[ROWS:, sj * COLS : (sj + 1) * COLS]
        turned.append(jnp.concatenate([real * cos + imag * sin, imag * cos - real * sin], axis=1))
    turned = jnp.concatenate(turned, axis=0)
    high = turned.astype(BF16)
    low = (turned - high.astype(F32)).astype(BF16)
    out = lax.dot_general(
        second[...],
        jnp.concatenate([high, low, high], axis=1),
        (((1,), (1,)), ((), ())),
        preferred_element_type=F32,
    )
    quarter = lax.broadcasted_iota(jnp.int32, (ROWS, COLS), 1) // ROWS
    for part in range(2):
        for half in range(2):
            block = [
                out[(part * 4 + r) * 32 : (part * 4 + r + 1) * 32, half * 128 : (half + 1) * 128]
                for r in range(4)
            ]
            for b in range(4):
                moved = [
                    block[r] if r == b else pltpu.roll(block[r], 32 * ((r - b) % 4), 1)
                    for r in range(4)
                ]
                spec = jnp.where(
                    quarter < 2,
                    jnp.where(quarter == 0, moved[0], moved[1]),
                    jnp.where(quarter == 2, moved[2], moved[3]),
                )
                index = part * 8 + half * 4 + b
                by_row[index * 32 : (index + 1) * 32, :] = spec.astype(BF16)
                mixed[pl.ds(index, 32, stride=16), :] = spec
    by_tile[...] = mixed[...].astype(BF16)


def spectra(past, *prepared):
    return pl.pallas_call(
        spectra_kernel,
        out_shape=[jax.ShapeDtypeStruct((512, COLS), BF16)] * 2,
        in_specs=[VMEM] * 6,
        out_specs=[VMEM] * 2,
        scratch_shapes=[pltpu.VMEM((512, COLS), F32)],
        compiler_params=pltpu.CompilerParams(vmem_limit_bytes=32 << 20),
        cost_estimate=pl.CostEstimate(flops=120_000_000, bytes_accessed=900_000, transcendentals=0),
    )(past, *prepared)


def pick_kernel(peers, roots, pieces, out):
    for k in range(STEPS):
        piece = pieces[pl.ds(pl.multiple_of(roots[k] * 16, 16), 16), :]
        for peer in range(peers):
            out[peer * 64 + k * 16 : peer * 64 + (k + 1) * 16, :] = piece


def pick(roots, pieces, peers):
    return pl.pallas_call(
        lambda *refs: pick_kernel(peers, *refs),
        out_shape=jax.ShapeDtypeStruct((peers * 64, COLS), BF16),
        in_specs=[SMEM, VMEM],
        out_specs=VMEM,
        compiler_params=pltpu.CompilerParams(vmem_limit_bytes=32 << 20),
        cost_estimate=pl.CostEstimate(flops=0, bytes_accessed=400_000, transcendentals=0),
    )(roots, pieces)


def correlate_kernel(numbers, own, near, far, out, mine, theirs):
    core = numbers[STEPS + 1]
    for place, block in ((core, near), (1 - core, far)):
        for peer in range(16):
            start = pl.multiple_of((2 * peer + place) * 64, 64)
            theirs[pl.ds(start, 64), :] = block[peer * 64 : (peer + 1) * 64, :].astype(F32)
    count = numbers[STEPS]
    weight = 1.0 / jnp.full((8, COLS), count, jnp.int32).astype(F32)
    nothing = jnp.zeros((8, COLS), F32)
    for j in range(4):
        scale = jnp.concatenate([jnp.where(j < count, weight, nothing)] * 4, axis=0)
        for ps in range(4):
            rows = slice((ps * 4 + j) * 32, (ps * 4 + j + 1) * 32)
            mine[rows, :] = own[rows, :].astype(F32) * scale
    for block in range(4):
        left = [
            mine[i * 32 + block * 8 : i * 32 + block * 8 + 8, :] for i in range(16)
        ]
        for k in range(STEPS):
            for q in range(2):
                start = block * 8 * 64 + k * 16 + q * 4
                real = [theirs[pl.ds(start + j, 8, stride=64), :] for j in range(4)]
                imag = [theirs[pl.ds(start + 8 + j, 8, stride=64), :] for j in range(4)]
                for s in range(2):
                    vis_real, vis_imag = nothing, nothing
                    for j in range(4):
                        a, b = left[s * 4 + j], left[8 + s * 4 + j]
                        vis_real = vis_real + (a * real[j] + b * imag[j])
                        vis_imag = vis_imag + (b * real[j] - a * imag[j])
                    at = (k * 2 + s) * 64 + block * 16 + q
                    out[pl.ds(at, 8, stride=2), :] = vis_real
                    out[pl.ds(512 + at, 8, stride=2), :] = vis_imag


def correlate(numbers, own, near, far):
    return pl.pallas_call(
        correlate_kernel,
        out_shape=jax.ShapeDtypeStruct((1024, COLS), F32),
        in_specs=[SMEM, VMEM, VMEM, VMEM],
        out_specs=VMEM,
        scratch_shapes=[pltpu.VMEM((512, COLS), F32), pltpu.VMEM((2048, COLS), F32)],
        compiler_params=pltpu.CompilerParams(vmem_limit_bytes=32 << 20),
        cost_estimate=pl.CostEstimate(flops=4_000_000, bytes_accessed=1_200_000, transcendentals=0),
    )(numbers, own, near, far)


def local(samples, valid_spectra, root_blocks):
    blocks, places = lax.axis_size("tm"), lax.axis_size("stn")
    tails, rows = tails_of(samples)
    past = lax.ppermute(tails, "tm", [(b, b + 1) for b in range(blocks - 1)])
    *prepared, numbers = ready(rows, valid_spectra, root_blocks, samples.shape[3])
    by_tile, by_row = spectra(past, *prepared)
    pieces = lax.all_to_all(by_tile, "stn", 0, 0, tiled=True)
    picked = pick(numbers, pieces, places // 2)
    same_core = [[2 * p + c for p in range(places // 2)] for c in range(2)]
    near = lax.all_to_all(picked, "stn", 0, 0, axis_index_groups=same_core, tiled=True)
    far = lax.ppermute(near, "stn", [(d, d ^ 1) for d in range(places)])
    vis = correlate(numbers, by_row, near, far)
    vis = vis.reshape(2, STEPS, 2, 32, 2, COLS).transpose(0, 1, 2, 4, 3, 5)
    return vis.reshape(1, 2, STEPS, 2, 2, 32 * COLS)


def solution(mesh):
    return jax.shard_map(
        local,
        mesh=mesh,
        in_specs=(P(None, "stn", "tm", None), P("tm"), P()),
        out_specs=P("tm", None, None, "stn", None, None),
        check_vma=False,
    )
```

```python
import math

import jax
import jax.numpy as jnp
import ml_dtypes
import numpy as np
from jax import lax
from jax.experimental import pallas as pl
from jax.experimental.pallas import tpu as pltpu
from jax.sharding import PartitionSpec as P

TAPS = 4
STEPS = 4
ROWS = 32
COLS = 128
F32, BF16 = jnp.float32, jnp.bfloat16
VMEM = pl.BlockSpec(memory_space=pltpu.VMEM)
SMEM = pl.BlockSpec(memory_space=pltpu.SMEM)
HBM = pl.BlockSpec(memory_space=pltpu.HBM)


def split(table):
    high = table.astype(ml_dtypes.bfloat16)
    low = (table - high.astype(np.float64)).astype(ml_dtypes.bfloat16)
    return high, low


def tables(channels):
    position = np.arange(TAPS * channels, dtype=np.float64)
    middle = (position - 0.5 * TAPS * channels + 0.5) / channels
    window = 0.5 - 0.5 * np.cos(2.0 * np.pi * (position + 0.5) / (TAPS * channels))
    taps = (np.sinc(middle) * window).astype(np.float32).reshape(TAPS * ROWS, COLS)
    row, col = np.arange(ROWS), np.arange(COLS)
    angle = 2.0 * np.pi * (row[:, None] * row[None, :] % ROWS) / ROWS
    cos, sin = np.cos(angle), np.sin(angle)
    high, low = split(np.block([[cos, sin], [-sin, cos]]))
    first = np.concatenate([high, high, low], axis=1)
    angle = 2.0 * np.pi * (row[:, None] * col[None, :]) / channels
    twist = np.concatenate([np.cos(angle), np.sin(angle)]).astype(np.float32)
    out_col = (4 * np.arange(32)[None, :] + np.arange(4)[:, None]).reshape(-1)
    angle = 2.0 * np.pi * (out_col[:, None] * col[None, :] % COLS) / COLS
    scale = 1.0 / math.sqrt(channels)
    cos, sin = np.cos(angle) * scale, np.sin(angle) * scale
    high, low = split(np.block([[cos, sin], [-sin, cos]]))
    second = np.concatenate([high, high, low], axis=1)
    return taps, first, twist, second


def tails_kernel(samples, tails, rows, held, mixed, sems):
    copies = [
        pltpu.make_async_copy(samples.at[part, sig], held.at[part, sig], sems.at[part * 2 + sig])
        for part in range(2)
        for sig in range(2)
    ]
    for copy in copies:
        copy.start()
    for part in range(2):
        copies[part * 2].wait()
        copies[part * 2 + 1].wait()
        both = jnp.concatenate(
            [held[part, 0].astype(F32), held[part, 1].astype(F32)], axis=0
        )
        for tile in range(ROWS):
            start = (part * ROWS + tile) * 8
            mixed[start : start + 8, :] = both[:, tile * COLS : (tile + 1) * COLS]
        for sig in range(2):
            for frame in range(4):
                row = mixed[pl.ds(part * ROWS * 8 + sig * 4 + frame, ROWS, stride=8), :]
                index = part * 2 + sig
                rows[(index * 4 + frame) * 32 : (index * 4 + frame + 1) * 32, :] = row
                if frame > 0:
                    start = (index * 3 + frame - 1) * 32
                    tails[start : start + 32, :] = row.astype(BF16)


def far_off(x):
    return pltpu.with_memory_space_constraint(x, pltpu.HBM)


def tails_of(samples):
    return pl.pallas_call(
        tails_kernel,
        out_shape=[
            jax.ShapeDtypeStruct((384, COLS), BF16),
            jax.ShapeDtypeStruct((512, COLS), F32),
        ],
        in_specs=[HBM],
        out_specs=[VMEM] * 2,
        scratch_shapes=[
            pltpu.VMEM(samples.shape, BF16),
            pltpu.VMEM((512, COLS), F32),
            pltpu.SemaphoreType.DMA((4,)),
        ],
        compiler_params=pltpu.CompilerParams(vmem_limit_bytes=32 << 20),
        cost_estimate=pl.CostEstimate(flops=0, bytes_accessed=600_000, transcendentals=0),
    )(far_off(samples))


def ready_kernel(rows, valid, roots, taps, first, twist, second, part_sums, *rest):
    near, numbers, sems = rest[:4], rest[4], rest[5]
    copies = [
        pltpu.make_async_copy(table, place, sems.at[i])
        for i, (table, place) in enumerate(zip((taps, first, twist, second), near))
    ]
    for copy in copies:
        copy.start()
    for k in range(STEPS):
        numbers[k] = roots[k]
    numbers[STEPS] = valid[0]
    numbers[STEPS + 1] = lax.rem(lax.axis_index("stn"), 2)
    copies[0].wait()
    weights = [near[0][k * ROWS : (k + 1) * ROWS, :] for k in range(TAPS)]
    for index in range(4):
        frame = [rows[(index * 4 + f) * 32 : (index * 4 + f + 1) * 32, :] for f in range(4)]
        for j in range(4):
            total = weights[3 - j] * frame[0]
            for f in range(1, j + 1):
                total = total + weights[3 - j + f] * frame[f]
            part_sums[(index * 4 + j) * 32 : (index * 4 + j + 1) * 32, :] = total
    for copy in copies[1:]:
        copy.wait()


def ready(rows, valid, roots, channels):
    consts = [jnp.asarray(t) for t in tables(channels)]
    return pl.pallas_call(
        ready_kernel,
        out_shape=[jax.ShapeDtypeStruct((512, COLS), F32)]
        + [jax.ShapeDtypeStruct(c.shape, c.dtype) for c in consts]
        + [pltpu.SMEM((STEPS + 2,), jnp.int32)],
        in_specs=[VMEM, SMEM, SMEM] + [HBM] * 4,
        out_specs=[VMEM] * 5 + [SMEM],
        scratch_shapes=[pltpu.SemaphoreType.DMA((4,))],
        compiler_params=pltpu.CompilerParams(vmem_limit_bytes=32 << 20),
        cost_estimate=pl.CostEstimate(flops=700_000, bytes_accessed=900_000, transcendentals=0),
    )(rows, valid, roots, *map(far_off, consts))


def spectra_kernel(past, part_sums, taps, first, twist, second, by_tile, by_row, mixed):
    weights = [taps[k * ROWS : (k + 1) * ROWS, :] for k in range(TAPS)]
    columns = []
    for sig in range(2):
        both = []
        for part in range(2):
            index = part * 2 + sig
            frame = [
                past[(index * 3 + f) * 32 : (index * 3 + f + 1) * 32, :].astype(F32)
                for f in range(3)
            ]
            sums = [
                part_sums[(index * 4 + j) * 32 : (index * 4 + j + 1) * 32, :] for j in range(4)
            ]
            for j in range(3):
                for k in range(3 - j):
                    sums[j] = sums[j] + weights[k] * frame[j + k]
            both.append(sums)
        for j in range(4):
            columns.append(jnp.concatenate([both[0][j], both[1][j]], axis=0))
    filt = jnp.concatenate(columns, axis=1)
    high = filt.astype(BF16)
    low = (filt - high.astype(F32)).astype(BF16)
    mid = jnp.dot(
        first[...], jnp.concatenate([high, low, high], axis=0), preferred_element_type=F32
    )
    cos, sin = twist[:ROWS, :], twist[ROWS:, :]
    turned = []
    for sj in range(8):
        real = mid[:ROWS, sj * COLS : (sj + 1) * COLS]
        imag = mid[ROWS:, sj * COLS : (sj + 1) * COLS]
        turned.append(jnp.concatenate([real * cos + imag * sin, imag * cos - real * sin], axis=1))
    turned = jnp.concatenate(turned, axis=0)
    high = turned.astype(BF16)
    low = (turned - high.astype(F32)).astype(BF16)
    out = lax.dot_general(
        second[...],
        jnp.concatenate([high, low, high], axis=1),
        (((1,), (1,)), ((), ())),
        preferred_element_type=F32,
    )
    quarter = lax.broadcasted_iota(jnp.int32, (ROWS, COLS), 1) // ROWS
    for part in range(2):
        for half in range(2):
            block = [
                out[(part * 4 + r) * 32 : (part * 4 + r + 1) * 32, half * 128 : (half + 1) * 128]
                for r in range(4)
            ]
            for b in range(4):
                moved = [
                    block[r] if r == b else pltpu.roll(block[r], 32 * ((r - b) % 4), 1)
                    for r in range(4)
                ]
                spec = jnp.where(
                    quarter < 2,
                    jnp.where(quarter == 0, moved[0], moved[1]),
                    jnp.where(quarter == 2, moved[2], moved[3]),
                )
                index = part * 8 + half * 4 + b
                by_row[index * 32 : (index + 1) * 32, :] = spec.astype(BF16)
                mixed[pl.ds(index, 32, stride=16), :] = spec
    by_tile[...] = mixed[...].astype(BF16)


def spectra(past, *prepared):
    return pl.pallas_call(
        spectra_kernel,
        out_shape=[jax.ShapeDtypeStruct((512, COLS), BF16)] * 2,
        in_specs=[VMEM] * 6,
        out_specs=[VMEM] * 2,
        scratch_shapes=[pltpu.VMEM((512, COLS), F32)],
        compiler_params=pltpu.CompilerParams(vmem_limit_bytes=32 << 20),
        cost_estimate=pl.CostEstimate(flops=120_000_000, bytes_accessed=900_000, transcendentals=0),
    )(past, *prepared)


def pick_kernel(peers, roots, pieces, out):
    for k in range(STEPS):
        piece = pieces[pl.ds(pl.multiple_of(roots[k] * 16, 16), 16), :]
        for peer in range(peers):
            out[peer * 64 + k * 16 : peer * 64 + (k + 1) * 16, :] = piece


def pick(roots, pieces, peers):
    return pl.pallas_call(
        lambda *refs: pick_kernel(peers, *refs),
        out_shape=jax.ShapeDtypeStruct((peers * 64, COLS), BF16),
        in_specs=[SMEM, VMEM],
        out_specs=VMEM,
        compiler_params=pltpu.CompilerParams(vmem_limit_bytes=32 << 20),
        cost_estimate=pl.CostEstimate(flops=0, bytes_accessed=400_000, transcendentals=0),
    )(roots, pieces)


def correlate_kernel(numbers, own, near, far, out, mine, theirs):
    core = numbers[STEPS + 1]
    for place, block in ((core, near), (1 - core, far)):
        for peer in range(16):
            start = pl.multiple_of((2 * peer + place) * 64, 64)
            theirs[pl.ds(start, 64), :] = block[peer * 64 : (peer + 1) * 64, :].astype(F32)
    count = numbers[STEPS]
    weight = 1.0 / jnp.full((8, COLS), count, jnp.int32).astype(F32)
    nothing = jnp.zeros((8, COLS), F32)
    for j in range(4):
        scale = jnp.concatenate([jnp.where(j < count, weight, nothing)] * 4, axis=0)
        for ps in range(4):
            rows = slice((ps * 4 + j) * 32, (ps * 4 + j + 1) * 32)
            mine[rows, :] = own[rows, :].astype(F32) * scale
    for block in range(4):
        left = [
            mine[i * 32 + block * 8 : i * 32 + block * 8 + 8, :] for i in range(16)
        ]
        for k in range(STEPS):
            for q in range(2):
                start = block * 8 * 64 + k * 16 + q * 4
                real = [theirs[pl.ds(start + j, 8, stride=64), :] for j in range(4)]
                imag = [theirs[pl.ds(start + 8 + j, 8, stride=64), :] for j in range(4)]
                for s in range(2):
                    vis_real, vis_imag = nothing, nothing
                    for j in range(4):
                        a, b = left[s * 4 + j], left[8 + s * 4 + j]
                        vis_real = vis_real + (a * real[j] + b * imag[j])
                        vis_imag = vis_imag + (b * real[j] - a * imag[j])
                    at = (k * 2 + s) * 64 + block * 16 + q
                    out[pl.ds(at, 8, stride=2), :] = vis_real
                    out[pl.ds(512 + at, 8, stride=2), :] = vis_imag


def correlate(numbers, own, near, far):
    return pl.pallas_call(
        correlate_kernel,
        out_shape=jax.ShapeDtypeStruct((1024, COLS), F32),
        in_specs=[SMEM, VMEM, VMEM, VMEM],
        out_specs=VMEM,
        scratch_shapes=[pltpu.VMEM((512, COLS), F32), pltpu.VMEM((2048, COLS), F32)],
        compiler_params=pltpu.CompilerParams(vmem_limit_bytes=32 << 20),
        cost_estimate=pl.CostEstimate(flops=4_000_000, bytes_accessed=1_200_000, transcendentals=0),
    )(numbers, own, near, far)


def local(samples, valid_spectra, root_blocks):
    blocks, places = lax.axis_size("tm"), lax.axis_size("stn")
    tails, rows = tails_of(samples)
    past = lax.ppermute(tails, "tm", [(b, b + 1) for b in range(blocks - 1)])
    *prepared, numbers = ready(rows, valid_spectra, root_blocks, samples.shape[3])
    by_tile, by_row = spectra(past, *prepared)
    pieces = lax.all_to_all(by_tile, "stn", 0, 0, tiled=True)
    picked = pick(numbers, pieces, places // 2)
    same_core = [[2 * p + c for p in range(places // 2)] for c in range(2)]
    near = lax.all_to_all(picked, "stn", 0, 0, axis_index_groups=same_core, tiled=True)
    far = lax.ppermute(near, "stn", [(d, d ^ 1) for d in range(places)])
    vis = correlate(numbers, by_row, near, far)
    vis = vis.reshape(2, STEPS, 2, 32, 2, COLS).transpose(0, 1, 2, 4, 3, 5)
    return vis.reshape(1, 2, STEPS, 2, 2, 32 * COLS)


def solution(mesh):
    return jax.shard_map(
        local,
        mesh=mesh,
        in_specs=(P(None, "stn", "tm", None), P("tm"), P()),
        out_specs=P("tm", None, None, "stn", None, None),
        check_vma=False,
    )
```

```python
import math

import jax
import jax.numpy as jnp
import ml_dtypes
import numpy as np
from jax import lax
from jax.experimental import pallas as pl
from jax.experimental.pallas import tpu as pltpu
from jax.sharding import PartitionSpec as P

TAPS = 4
STEPS = 4
ROWS = 32
COLS = 128
F32, BF16 = jnp.float32, jnp.bfloat16
VMEM = pl.BlockSpec(memory_space=pltpu.VMEM)
SMEM = pl.BlockSpec(memory_space=pltpu.SMEM)
HBM = pl.BlockSpec(memory_space=pltpu.HBM)


def split(table):
    high = table.astype(ml_dtypes.bfloat16)
    low = (table - high.astype(np.float64)).astype(ml_dtypes.bfloat16)
    return high, low


def tables(channels):
    position = np.arange(TAPS * channels, dtype=np.float64)
    middle = (position - 0.5 * TAPS * channels + 0.5) / channels
    window = 0.5 - 0.5 * np.cos(2.0 * np.pi * (position + 0.5) / (TAPS * channels))
    taps = (np.sinc(middle) * window).astype(np.float32).reshape(TAPS * ROWS, COLS)
    row, col = np.arange(ROWS), np.arange(COLS)
    angle = 2.0 * np.pi * (row[:, None] * row[None, :] % ROWS) / ROWS
    cos, sin = np.cos(angle), np.sin(angle)
    high, low = split(np.block([[cos, sin], [-sin, cos]]))
    first = np.concatenate([high, high, low], axis=1)
    angle = 2.0 * np.pi * (row[:, None] * col[None, :]) / channels
    twist = np.concatenate([np.cos(angle), np.sin(angle)]).astype(np.float32)
    out_col = (4 * np.arange(32)[None, :] + np.arange(4)[:, None]).reshape(-1)
    angle = 2.0 * np.pi * (out_col[:, None] * col[None, :] % COLS) / COLS
    scale = 1.0 / math.sqrt(channels)
    cos, sin = np.cos(angle) * scale, np.sin(angle) * scale
    high, low = split(np.block([[cos, sin], [-sin, cos]]))
    second = np.concatenate([high, high, low], axis=1)
    return taps, first, twist, second


def near_copies(samples, held, sems, first):
    return [
        pltpu.make_async_copy(samples.at[part, sig], held.at[part, sig], sems.at[first + part * 2 + sig])
        for part in range(2)
        for sig in range(2)
    ]


def laid_out(part, held, mixed):
    both = jnp.concatenate([held[part, 0].astype(F32), held[part, 1].astype(F32)], axis=0)
    for tile in range(ROWS):
        start = (part * ROWS + tile) * 8
        mixed[start : start + 8, :] = both[:, tile * COLS : (tile + 1) * COLS]


def frame_of(part, sig, frame, mixed):
    return mixed[pl.ds(part * ROWS * 8 + sig * 4 + frame, ROWS, stride=8), :]


def tiles_kernel(samples, roots, by_tile, numbers, held, mixed, blocks, sems):
    copies = near_copies(samples, held, sems, 0)
    scalars = pltpu.make_async_copy(roots, blocks, sems.at[4])
    for copy in copies + [scalars]:
        copy.start()
    for part in range(2):
        copies[part * 2].wait()
        copies[part * 2 + 1].wait()
        both = jnp.concatenate([held[part, 0].astype(F32), held[part, 1].astype(F32)], axis=0)
        for tile in range(ROWS):
            start = tile * 16 + part * 8
            mixed[start : start + 8, :] = both[:, tile * COLS : (tile + 1) * COLS]
    by_tile[...] = mixed[...].astype(BF16)
    scalars.wait()
    for k in range(STEPS):
        numbers[k] = blocks[k]
    numbers[STEPS] = lax.axis_index("stn")


def far_off(x):
    return pltpu.with_memory_space_constraint(x, pltpu.HBM)


def tiles_of(samples, roots):
    return pl.pallas_call(
        tiles_kernel,
        out_shape=[
            jax.ShapeDtypeStruct((512, COLS), BF16),
            pltpu.SMEM((STEPS + 1,), jnp.int32),
        ],
        in_specs=[HBM] * 2,
        out_specs=[VMEM, SMEM],
        scratch_shapes=[
            pltpu.VMEM(samples.shape, BF16),
            pltpu.VMEM((512, COLS), F32),
            pltpu.SMEM((STEPS,), jnp.int32),
            pltpu.SemaphoreType.DMA((5,)),
        ],
        compiler_params=pltpu.CompilerParams(vmem_limit_bytes=32 << 20),
        cost_estimate=pl.CostEstimate(flops=0, bytes_accessed=600_000, transcendentals=0),
    )(far_off(samples), far_off(roots))


def ready_kernel(samples, valid, after, taps, first, twist, second, part_sums, tails, *rest):
    near, numbers, held, mixed, sems = rest[:4], *rest[4:]
    tables_in = [
        pltpu.make_async_copy(table, place, sems.at[i])
        for i, (table, place) in enumerate(zip((taps, first, twist, second), near))
    ]
    own_in = near_copies(samples, held, sems, 4)
    for copy in own_in + tables_in:
        copy.start()
    tables_in[0].wait()
    weights = [near[0][k * ROWS : (k + 1) * ROWS, :] for k in range(TAPS)]
    for part in range(2):
        own_in[part * 2].wait()
        own_in[part * 2 + 1].wait()
        laid_out(part, held, mixed)
        for sig in range(2):
            index = part * 2 + sig
            frame = [frame_of(part, sig, f, mixed) for f in range(4)]
            for f in range(1, 4):
                start = (index * 3 + f - 1) * 32
                tails[start : start + 32, :] = frame[f].astype(BF16)
            for j in range(4):
                total = weights[3 - j] * frame[0]
                for f in range(1, j + 1):
                    total = total + weights[3 - j + f] * frame[f]
                part_sums[(index * 4 + j) * 32 : (index * 4 + j + 1) * 32, :] = total
    for copy in tables_in[1:]:
        copy.wait()
    numbers[0] = valid[0]
    numbers[1] = lax.axis_index("stn")


def ready(samples, valid, after):
    consts = [jnp.asarray(t) for t in tables(samples.shape[3])]
    return pl.pallas_call(
        ready_kernel,
        out_shape=[
            jax.ShapeDtypeStruct((512, COLS), F32),
            jax.ShapeDtypeStruct((384, COLS), BF16),
        ]
        + [jax.ShapeDtypeStruct(c.shape, c.dtype) for c in consts]
        + [pltpu.SMEM((2,), jnp.int32)],
        in_specs=[HBM, SMEM, VMEM] + [HBM] * 4,
        out_specs=[VMEM] * 6 + [SMEM],
        scratch_shapes=[
            pltpu.VMEM(samples.shape, BF16),
            pltpu.VMEM((512, COLS), F32),
            pltpu.SemaphoreType.DMA((8,)),
        ],
        compiler_params=pltpu.CompilerParams(vmem_limit_bytes=32 << 20),
        cost_estimate=pl.CostEstimate(flops=700_000, bytes_accessed=900_000, transcendentals=0),
    )(far_off(samples), valid, after, *map(far_off, consts))


def transform(filt, exact, first, twist, second):
    high = filt.astype(BF16)
    if exact:
        mid = jnp.dot(first[:, :64], high, preferred_element_type=F32) + jnp.dot(
            first[:, 128:], high, preferred_element_type=F32
        )
    else:
        low = (filt - high.astype(F32)).astype(BF16)
        mid = jnp.dot(
            first[...], jnp.concatenate([high, low, high], axis=0), preferred_element_type=F32
        )
    cos, sin = twist[:ROWS, :], twist[ROWS:, :]
    turned = []
    for sj in range(8):
        real = mid[:ROWS, sj * COLS : (sj + 1) * COLS]
        imag = mid[ROWS:, sj * COLS : (sj + 1) * COLS]
        turned.append(jnp.concatenate([real * cos + imag * sin, imag * cos - real * sin], axis=1))
    turned = jnp.concatenate(turned, axis=0)
    high = turned.astype(BF16)
    low = (turned - high.astype(F32)).astype(BF16)
    out = lax.dot_general(
        second[...],
        jnp.concatenate([high, low, high], axis=1),
        (((1,), (1,)), ((), ())),
        preferred_element_type=F32,
    )
    quarter = lax.broadcasted_iota(jnp.int32, (ROWS, COLS), 1) // ROWS
    spectra_of = []
    for part in range(2):
        for half in range(2):
            block = [
                out[(part * 4 + r) * 32 : (part * 4 + r + 1) * 32, half * 128 : (half + 1) * 128]
                for r in range(4)
            ]
            for b in range(4):
                moved = [
                    block[r] if r == b else pltpu.roll(block[r], 32 * ((r - b) % 4), 1)
                    for r in range(4)
                ]
                spec = jnp.where(
                    quarter < 2,
                    jnp.where(quarter == 0, moved[0], moved[1]),
                    jnp.where(quarter == 2, moved[2], moved[3]),
                )
                spectra_of.append(spec)
    return spectra_of


def own_kernel(past, after, part_sums, taps, first, twist, second, by_row):
    weights = [taps[k * ROWS : (k + 1) * ROWS, :] for k in range(TAPS)]
    columns = []
    for sig in range(2):
        both = []
        for part in range(2):
            index = part * 2 + sig
            frame = [
                past[(index * 3 + f) * 32 : (index * 3 + f + 1) * 32, :].astype(F32)
                for f in range(3)
            ]
            sums = [
                part_sums[(index * 4 + j) * 32 : (index * 4 + j + 1) * 32, :] for j in range(4)
            ]
            for j in range(3):
                for k in range(3 - j):
                    sums[j] = sums[j] + weights[k] * frame[j + k]
            both.append(sums)
        for j in range(4):
            columns.append(jnp.concatenate([both[0][j], both[1][j]], axis=0))
    filt = jnp.concatenate(columns, axis=1)
    for index, spec in enumerate(transform(filt, False, first, twist, second)):
        by_row[index * 32 : (index + 1) * 32, :] = spec.astype(BF16)


def own_spectra(past, *prepared):
    return pl.pallas_call(
        own_kernel,
        out_shape=jax.ShapeDtypeStruct((512, COLS), BF16),
        in_specs=[VMEM] * 7,
        out_specs=VMEM,
        compiler_params=pltpu.CompilerParams(vmem_limit_bytes=32 << 20),
        cost_estimate=pl.CostEstimate(flops=14_000_000_000, bytes_accessed=900_000, transcendentals=0),
    )(past, *prepared)


def pick_kernel(numbers, pieces, out):
    for k in range(STEPS):
        out[k * 16 : (k + 1) * 16, :] = pieces[pl.ds(pl.multiple_of(numbers[k] * 16, 16), 16), :]


def pick(numbers, pieces):
    return pl.pallas_call(
        pick_kernel,
        out_shape=jax.ShapeDtypeStruct((64, COLS), BF16),
        in_specs=[SMEM, VMEM],
        out_specs=VMEM,
        compiler_params=pltpu.CompilerParams(vmem_limit_bytes=32 << 20),
        cost_estimate=pl.CostEstimate(flops=0, bytes_accessed=150_000, transcendentals=0),
    )(numbers, pieces)


def filter_kernel(peers, numbers, picked, past, taps, out):
    weights = [
        jnp.broadcast_to(taps[pl.ds(numbers[1] + k * ROWS, 1), :], (8, COLS)) for k in range(TAPS)
    ]
    frame = lax.broadcasted_iota(jnp.int32, (8, COLS), 0) % 4
    now, before = picked[...].astype(F32), past[...].astype(F32)
    rows = []
    for start in range(0, 64, 8):
        mine, old = now[start : start + 8, :], before[start : start + 8, :]
        total = weights[3] * mine
        for k in range(3):
            moved = jnp.where(
                frame >= 3 - k, pltpu.roll(mine, 3 - k, 0), pltpu.roll(old, 7 - k, 0)
            )
            total = total + weights[k] * moved
        rows.append(total)
    rows = jnp.concatenate(rows, axis=0).astype(BF16)
    for peer in range(peers):
        out[peer * 64 : (peer + 1) * 64, :] = rows


def filter_tiles(numbers, picked, past, taps, peers):
    return pl.pallas_call(
        lambda *refs: filter_kernel(peers, *refs),
        out_shape=jax.ShapeDtypeStruct((peers * 64, COLS), BF16),
        in_specs=[SMEM, VMEM, VMEM, VMEM],
        out_specs=VMEM,
        compiler_params=pltpu.CompilerParams(vmem_limit_bytes=32 << 20),
        cost_estimate=pl.CostEstimate(flops=100_000, bytes_accessed=400_000, transcendentals=0),
    )(numbers, picked, past, taps)


def roots_kernel(both, first, twist, second, spectra, theirs):
    for core in range(2):
        for peer in range(16):
            start, at = (2 * peer + core) * 64, (core * 16 + peer) * 64
            theirs[start : start + 64, :] = both[at : at + 64, :].astype(F32)
    for k in range(STEPS):
        filt = jnp.concatenate(
            [
                jnp.concatenate(
                    [theirs[pl.ds(k * 16 + part * 8 + sj, ROWS, stride=64), :] for sj in range(8)],
                    axis=1,
                )
                for part in range(2)
            ],
            axis=0,
        )
        for index, spec in enumerate(transform(filt, True, first, twist, second)):
            at = (k * 16 + index) * 32
            spectra[at : at + 32, :] = spec


def root_spectra(both, *tables_near):
    return pl.pallas_call(
        roots_kernel,
        out_shape=jax.ShapeDtypeStruct((2048, COLS), F32),
        in_specs=[VMEM] * 4,
        out_specs=VMEM,
        scratch_shapes=[pltpu.VMEM((2048, COLS), F32)],
        compiler_params=pltpu.CompilerParams(vmem_limit_bytes=32 << 20),
        cost_estimate=pl.CostEstimate(flops=500_000_000, bytes_accessed=1_500_000, transcendentals=0),
    )(both, *tables_near)


def correlate_kernel(numbers, own, spectra, out, mine):
    count = numbers[0]
    weight = 1.0 / jnp.full((ROWS, COLS), count, jnp.int32).astype(F32)
    nothing = jnp.zeros((ROWS, COLS), F32)
    for j in range(4):
        scale = jnp.where(j < count, weight, nothing)
        for ps in range(4):
            rows = slice((ps * 4 + j) * 32, (ps * 4 + j + 1) * 32)
            mine[rows, :] = own[rows, :].astype(F32) * scale
    for k in range(STEPS):
        for s in range(2):
            for q in range(2):
                vis_real, vis_imag = nothing, nothing
                for j in range(4):
                    at = (s * 4 + j) * 32
                    a, b = mine[at : at + 32, :], mine[256 + at : 288 + at, :]
                    at = (k * 16 + q * 4 + j) * 32
                    real, imag = spectra[at : at + 32, :], spectra[256 + at : 288 + at, :]
                    vis_real = vis_real + (a * real + b * imag)
                    vis_imag = vis_imag + (b * real - a * imag)
                at = (k * 2 + s) * 64 + q
                out[pl.ds(at, ROWS, stride=2), :] = vis_real
                out[pl.ds(512 + at, ROWS, stride=2), :] = vis_imag


def correlate(numbers, own, spectra):
    return pl.pallas_call(
        correlate_kernel,
        out_shape=jax.ShapeDtypeStruct((1024, COLS), F32),
        in_specs=[SMEM, VMEM, VMEM],
        out_specs=VMEM,
        scratch_shapes=[pltpu.VMEM((512, COLS), F32)],
        compiler_params=pltpu.CompilerParams(vmem_limit_bytes=32 << 20),
        cost_estimate=pl.CostEstimate(flops=4_000_000, bytes_accessed=1_500_000, transcendentals=0),
    )(numbers, own, spectra)


def local(samples, valid_spectra, root_blocks):
    blocks, places = lax.axis_size("tm"), lax.axis_size("stn")
    onward = [(b, b + 1) for b in range(blocks - 1)]
    same_core = [[2 * p + c for p in range(places // 2)] for c in range(2)]
    by_tile, roots = tiles_of(samples, root_blocks)
    pieces = lax.all_to_all(by_tile, "stn", 0, 0, tiled=True)
    picked = pick(roots, pieces)
    picked_past = lax.ppermute(picked, "tm", onward)
    part_sums, tails, taps, first, twist, second, numbers = ready(samples, valid_spectra, picked)
    past = lax.ppermute(tails, "tm", onward)
    tiles = filter_tiles(numbers, picked, picked_past, taps, places // 2)
    near = lax.all_to_all(tiles, "stn", 0, 0, axis_index_groups=same_core, tiled=True)
    pairs = [[2 * p, 2 * p + 1] for p in range(places // 2)]
    both = lax.all_gather(near, "stn", axis_index_groups=pairs)
    roots_near = root_spectra(both.reshape(-1, COLS), first, twist, second)
    own = own_spectra(past, roots_near, part_sums, taps, first, twist, second)
    vis = correlate(numbers, own, roots_near)
    vis = vis.reshape(2, STEPS, 2, 32, 2, COLS).transpose(0, 1, 2, 4, 3, 5)
    return vis.reshape(1, 2, STEPS, 2, 2, 32 * COLS)


def solution(mesh):
    return jax.shard_map(
        local,
        mesh=mesh,
        in_specs=(P(None, "stn", "tm", None), P("tm"), P()),
        out_specs=P("tm", None, None, "stn", None, None),
        check_vma=False,
    )
```
